128 devices in a mesh: dp: 64 (over z, x, y), col: 2 (over core).
Axes of the slice: x: 4, y: 4, z: 4, core: 2. Of those that a mesh axis runs over, the one named last changes fastest.
Arguments:
- embeddings: bfloat16 [327680, 4096], P('dp', 'col'), may hold values from -500 to 500
- start_basis: bfloat16 [4096, 128], P('col'), may hold values from -1 to 1
Outputs:
- projected: float32 [4096, 128], P('col')
- image_factor: float32 [128, 128], replicated
The draws below stay inside these ranges and needn't reach their ends.
All inputs are finite; a program needn't handle non-finite values.
Results may differ from the reference program's by a relative error of at most 0.0014.
Values may be sent and summed in bfloat16 or wider, within the bound.
A program may use at most 128 MiB of HBM per device.

```python
import jax
import jax.numpy as jnp
from jax import lax

D = 4096
K = 128
ROWS_DEV = 5120
ROWS = 327680
N_DP = 64


def draw_embeddings(key, part):
    key = jax.random.fold_in(key, 11)
    noise_key, row_key, column_key = jax.random.split(key, 3)
    position = (jnp.arange(ROWS, dtype=jnp.float32) / ROWS)[:, None]
    row_draw = jax.random.uniform(row_key, (ROWS, 1), jnp.float32)
    column_scale = 10.0 ** jax.random.uniform(column_key, (1, D), jnp.float32)
    row_scale = 10.0 ** (0.5 * row_draw + 0.75 * position - 0.25)
    noise = jnp.clip(jax.random.normal(noise_key, (ROWS, D), jnp.float32), -4.0, 4.0)
    values = row_scale * column_scale * noise
    return values.astype(jnp.bfloat16)


def draw_start_basis(key, part):
    key = jax.random.fold_in(key, 23)
    shared_key, noise_key, spread_key = jax.random.split(key, 3)
    exponent = jax.random.uniform(spread_key, (1, K), jnp.float32, -2.4, -0.4)
    spread = 10.0 ** exponent
    shared = jnp.clip(jax.random.normal(shared_key, (D, 1), jnp.float32), -4.0, 4.0)
    noise = jnp.clip(jax.random.normal(noise_key, (D, K), jnp.float32), -4.0, 4.0)
    values = (shared + spread * noise) * D ** (-0.5)
    return values.astype(jnp.bfloat16)


def setup_inputs(seed: int = 0) -> dict:
    streams_of = jax.random.split(jax.random.key(seed), 3)
    embeddings = draw_embeddings(jax.random.fold_in(streams_of[2], 71), 0)
    start_basis = draw_start_basis(jax.random.fold_in(streams_of[2], 71), 0)
    return {"embeddings": embeddings, "start_basis": start_basis}


def gram_matrix(rows_in):
    return lax.dot_general(rows_in.astype(jnp.float32), rows_in.astype(jnp.float32), (((0,), (0,)), ((), ())), precision=lax.Precision.HIGHEST, preferred_element_type=jnp.float32)

def whiten(rows_in, total):
    factor = jnp.linalg.cholesky(total)
    identity = jnp.eye(total.shape[0], dtype=total.dtype)
    inverse = lax.linalg.triangular_solve(factor, identity, left_side=True, lower=True)
    whitened = lax.dot_general(rows_in.astype(jnp.float32), inverse.astype(jnp.float32), (((1,), (1,)), ((), ())), precision=lax.Precision.HIGHEST, preferred_element_type=jnp.float32)
    return (whitened, factor)

def reference(embeddings, start_basis):
    blocks = embeddings.reshape(N_DP, ROWS_DEV, D)

    def image_block(block):
        return jnp.dot(block.astype(jnp.float32), start_basis.astype(jnp.float32), preferred_element_type=jnp.float32)
    image_rows = lax.map(image_block, blocks).reshape(ROWS, K)
    ortho_rows, first_factor = whiten(image_rows, gram_matrix(image_rows))
    final_rows, unused_factor = whiten(ortho_rows, gram_matrix(ortho_rows))
    final_basis = final_rows.astype(jnp.bfloat16)
    final_blocks = final_basis.reshape(N_DP, ROWS_DEV, K)

    def accumulate(carry, pair):
        block, piece = pair
        return (carry + lax.dot_general(block.astype(jnp.float32), piece.astype(jnp.float32), (((0,), (0,)), ((), ())), preferred_element_type=jnp.float32), None)
    total, unused = lax.scan(accumulate, jnp.zeros((D, K), jnp.float32), (blocks, final_blocks))
    return (total * ROWS ** (-0.5), first_factor * ROWS ** (-0.5))
```

```python
import functools

import jax
import jax.numpy as jnp
from jax import lax
from jax.experimental import pallas as pl
from jax.experimental.pallas import tpu as pltpu
from jax.sharding import PartitionSpec as P

F32 = jnp.float32
BF16 = jnp.bfloat16
MESH = pl.DeviceIdType.MESH
CHUNK = 512
BLOCK = 512
LAG = 2


def stride_of(dim):
    return 1 + 3 * dim + 9 * ((dim * (dim - 1)) // 2)


def reduce_kernel(
    a_hbm, q_hbm, t_ref, qf_ref,
    a_v, p_own, p_other, img, t_own, r1, r2, r3, acc1, acc2,
    load_sem, q_sem, ps_sem, pr_sem, s_sem, r_sem, hs_sem, hr_sem, qs_sem, qr_sem,
):
    rows, cols = a_v.shape
    n_chunk = rows // CHUNK
    n_block = cols // BLOCK
    dp = lax.axis_index("dp")
    core = lax.axis_index("col")

    def load(i):
        sl = pl.ds(pl.multiple_of(i * CHUNK, CHUNK), CHUNK)
        return pltpu.make_async_copy(a_hbm.at[sl], a_v.at[sl], load_sem.at[i])

    q_copy = pltpu.make_async_copy(q_hbm, qf_ref.at[core], q_sem)
    q_copy.start()
    for i in range(n_chunk):
        load(i).start()

    sibling = {"dp": dp, "col": 1 - core}

    def peer(dim, offset):
        stride = stride_of(dim)
        me = (dp // stride) % 4
        to = (me + offset) % 4
        return to, {"dp": dp + (to - me) * stride, "col": core}

    barrier = pltpu.get_barrier_semaphore()
    pl.semaphore_signal(barrier, inc=1, device_id=sibling, device_id_type=MESH)
    for dim in range(3):
        for offset in range(1, 4):
            pl.semaphore_signal(
                barrier, inc=1, device_id=peer(dim, offset)[1], device_id_type=MESH
            )
    pl.semaphore_wait(barrier, 10)

    q_copy.wait()
    q_send = pltpu.make_async_remote_copy(
        src_ref=qf_ref.at[core], dst_ref=qf_ref.at[core], send_sem=qs_sem, recv_sem=qr_sem,
        device_id=sibling, device_id_type=MESH,
    )
    q_send.start()

    def p_copy(i):
        sl = pl.ds(pl.multiple_of(i * CHUNK, CHUNK), CHUNK)
        return pltpu.make_async_remote_copy(
            src_ref=p_own.at[sl], dst_ref=p_other.at[sl],
            send_sem=ps_sem.at[i], recv_sem=pr_sem.at[i],
            device_id=sibling, device_id_type=MESH,
        )

    def multiply(i):
        sl = pl.ds(pl.multiple_of(i * CHUNK, CHUNK), CHUNK)
        p_own[sl] = jnp.dot(a_v[sl], qf_ref[core], preferred_element_type=F32)

    def combine(i):
        sl = pl.ds(pl.multiple_of(i * CHUNK, CHUNK), CHUNK)
        total = (p_own[sl] + p_other[sl]).T
        high = total.astype(BF16)
        img[0:128, sl] = high
        img[128:256, sl] = (total - high.astype(F32)).astype(BF16)

    for i in range(LAG):
        load(i).wait()
        multiply(i)
        p_copy(i).start()

    def step(i, carry):
        load(i).wait()
        p_copy(i - LAG).wait_recv()
        multiply(i)
        combine(i - LAG)
        p_copy(i).start()
        return carry

    lax.fori_loop(LAG, n_chunk, step, 0)
    for i in range(n_chunk - LAG, n_chunk):
        p_copy(i).wait_recv()
        combine(i)

    def dims(b):
        first = (2 * b + core) % 3
        return [(first + s) % 3 for s in range(3)]

    def position(dim):
        return (dp // stride_of(dim)) % 4

    def send(b, stage, offset):
        dim = dims(b)
        pos = [position(d) for d in dim]
        level = stage if stage < 3 else 5 - stage
        to, device = peer(dim[level], offset)
        c0 = b * BLOCK
        if stage == 0:
            src = t_own.at[pl.ds(pl.multiple_of(to * 32, 32), 32), pl.ds(c0, BLOCK)]
            dst = r1.at[b, offset - 1]
        elif stage == 1:
            src = acc1.at[b, pl.ds(pl.multiple_of(to * 8, 8), 8)]
            dst = r2.at[b, offset - 1]
        elif stage == 2:
            src = acc2.at[b, :, pl.ds(pl.multiple_of(to * 128, 128), 128)]
            dst = r3.at[b, offset - 1]
        else:
            if stage == 3:
                rsl = pl.ds(pl.multiple_of(pos[0] * 32 + pos[1] * 8, 8), 8)
                csl = pl.ds(pl.multiple_of(c0 + pos[2] * 128, 128), 128)
            elif stage == 4:
                rsl = pl.ds(pl.multiple_of(pos[0] * 32 + pos[1] * 8, 8), 8)
                csl = pl.ds(c0, BLOCK)
            else:
                rsl = pl.ds(pl.multiple_of(pos[0] * 32, 32), 32)
                csl = pl.ds(c0, BLOCK)
            src = t_ref.at[core, rsl, csl]
            dst = t_ref.at[core, rsl, csl]
        return pltpu.make_async_remote_copy(
            src_ref=src, dst_ref=dst,
            send_sem=s_sem.at[b, stage, offset - 1], recv_sem=r_sem.at[b, stage, offset - 1],
            device_id=device, device_id_type=MESH,
        )

    def half(b):
        piece = t_ref.at[core, :, pl.ds(b * BLOCK, BLOCK)]
        return pltpu.make_async_remote_copy(
            src_ref=piece, dst_ref=piece, send_sem=hs_sem.at[b], recv_sem=hr_sem.at[b],
            device_id=sibling, device_id_type=MESH,
        )

    def start(b, stage):
        for offset in range(1, 4):
            send(b, stage, offset).start()

    def receive(b, stage):
        for offset in range(1, 4):
            send(b, stage, offset).wait_recv()

    def advance(b, stage):
        dim = dims(b)
        pos = [position(d) for d in dim]
        c0 = b * BLOCK
        receive(b, stage)
        if stage == 0:
            own = t_own[pl.ds(pl.multiple_of(pos[0] * 32, 32), 32), pl.ds(c0, BLOCK)]
            acc1[b] = (own + r1[b, 0]) + (r1[b, 1] + r1[b, 2])
        elif stage == 1:
            own = acc1[b, pl.ds(pl.multiple_of(pos[1] * 8, 8), 8)]
            acc2[b] = (own + r2[b, 0]) + (r2[b, 1] + r2[b, 2])
        elif stage == 2:
            own = acc2[b, :, pl.ds(pl.multiple_of(pos[2] * 128, 128), 128)]
            rsl = pl.ds(pl.multiple_of(pos[0] * 32 + pos[1] * 8, 8), 8)
            csl = pl.ds(pl.multiple_of(c0 + pos[2] * 128, 128), 128)
            t_ref[core, rsl, csl] = (own + r3[b, 0]) + (r3[b, 1] + r3[b, 2])
        if stage < 5:
            start(b, stage + 1)
        else:
            half(b).start()

    for turn in range(n_block + 6):
        if turn < n_block:
            csl = pl.ds(turn * BLOCK, BLOCK)
            both = jnp.dot(img[...], a_v[:, csl], preferred_element_type=F32)
            t_own[:, csl] = both[0:128] + both[128:256]
            start(turn, 0)
        for b in range(n_block):
            stage = turn - 1 - b
            if 0 <= stage < 6:
                advance(b, stage)

    for b in range(n_block):
        half(b).wait_recv()
    q_send.wait()
    for i in range(n_chunk):
        p_copy(i).wait_send()
    for b in range(n_block):
        for stage in range(6):
            for offset in range(1, 4):
                send(b, stage, offset).wait_send()
        half(b).wait_send()


def split3(x):
    high = x.astype(BF16)
    rest = x - high.astype(F32)
    mid = rest.astype(BF16)
    low = (rest - mid.astype(F32)).astype(BF16)
    return jnp.concatenate([high, mid, low], 0)


def fold3(x):
    n = x.shape[0] // 3
    return x[0:n] + (x[n : 2 * n] + x[2 * n :])


def factor_and_inverse(gram, want_factor, step=8):
    n = gram.shape[0]
    gram = 0.5 * (gram + gram.T)
    lane = lax.broadcasted_iota(jnp.int32, (n, n), 1)
    row = lax.broadcasted_iota(jnp.int32, (n, n), 0)
    rest = gram
    inverse = []
    factor = None
    for c0 in range(0, n, step):
        m_rows = n - c0
        cols = [
            jnp.broadcast_to(rest[:, c0 + k : c0 + k + 1], (m_rows, n)) for k in range(step)
        ]
        ln = lane[c0:]
        rw = row[:m_rows]
        eye = jnp.where(ln == rw + c0, 1.0, 0.0).astype(F32)
        rest = jnp.where((ln >= c0) & (ln < c0 + step), eye, rest)
        scale = jnp.zeros((step, n), F32)
        part = jnp.zeros((m_rows, n), F32)
        for k in range(step):
            pivot = cols[k][k : k + 1]
            root = lax.rsqrt(pivot)
            scale = jnp.where(rw[:step] == k, root, scale)
            if want_factor:
                part = jnp.where((ln == c0 + k) & (rw >= k), cols[k] * root, part)
            mult = jnp.where(rw > k, cols[k] * (1.0 / pivot), 0.0)
            for later in range(k + 1, step):
                cols[later] = cols[later] - mult * cols[later][k : k + 1]
            rest = rest - mult * rest[k : k + 1]
        inverse.append(rest[:step] * scale)
        if want_factor:
            if c0:
                part = jnp.concatenate([factor[:c0], factor[c0:] + part], 0)
            factor = part
        rest = rest[step:]
    inverse = jnp.where(lane <= row, jnp.concatenate(inverse, 0), 0.0)
    return inverse, factor


def small_kernel(row_factor, t_ref, q_ref, out_ref, factor_ref, s_ref, w_ref):
    nt = (((1,), (1,)), ((), ()))
    core = lax.axis_index("col")
    gram = jnp.zeros((128, 128), F32)
    for c in range(2):
        gram += fold3(jnp.dot(split3(t_ref[c]), q_ref[c], preferred_element_type=F32))
    inverse, factor = factor_and_inverse(gram, True)
    factor_ref[...] = factor * row_factor
    gram = jnp.zeros((128, 128), F32)
    inverse3 = split3(inverse)
    for c in range(2):
        s_ref[c] = jnp.dot(
            inverse, t_ref[c], precision=lax.Precision.HIGHEST, preferred_element_type=F32
        )
        w_ref[...] = fold3(
            lax.dot_general(inverse3, q_ref[c], nt, preferred_element_type=F32)
        )
        gram += lax.dot_general(
            s_ref[c], w_ref[...], nt, precision=lax.Precision.HIGHEST, preferred_element_type=F32
        )
    inverse, _ = factor_and_inverse(gram, False)
    final = jnp.dot(
        inverse * row_factor, s_ref[core], precision=lax.Precision.HIGHEST,
        preferred_element_type=F32,
    )
    out_ref[...] = final.T


def on_device(embeddings, start_basis):
    rows, cols = embeddings.shape
    k = start_basis.shape[1]
    n_block = cols // BLOCK
    n_chunk = rows // CHUNK
    row_factor = (rows * lax.axis_size("dp")) ** (-0.5)
    vmem = pl.BlockSpec(memory_space=pltpu.VMEM)
    anywhere = pl.BlockSpec(memory_space=pl.ANY)
    dma = pltpu.SemaphoreType.DMA
    total, basis = pl.pallas_call(
        reduce_kernel,
        out_shape=[
            jax.ShapeDtypeStruct((2, k, cols), F32),
            jax.ShapeDtypeStruct((2, cols, k), BF16),
        ],
        in_specs=[anywhere, anywhere],
        out_specs=[vmem, vmem],
        scratch_shapes=[
            pltpu.VMEM((rows, cols), BF16),
            pltpu.VMEM((rows, k), F32),
            pltpu.VMEM((rows, k), F32),
            pltpu.VMEM((2 * k, rows), BF16),
            pltpu.VMEM((k, cols), F32),
            pltpu.VMEM((n_block, 3, 32, BLOCK), F32),
            pltpu.VMEM((n_block, 3, 8, BLOCK), F32),
            pltpu.VMEM((n_block, 3, 8, 128), F32),
            pltpu.VMEM((n_block, 32, BLOCK), F32),
            pltpu.VMEM((n_block, 8, BLOCK), F32),
            dma((n_chunk,)), dma, dma((n_chunk,)), dma((n_chunk,)),
            dma((n_block, 6, 3)), dma((n_block, 6, 3)),
            dma((n_block,)), dma((n_block,)), dma, dma,
        ],
        compiler_params=pltpu.CompilerParams(
            collective_id=0, has_side_effects=True, vmem_limit_bytes=48 * 2**20
        ),
        name="image_and_sum",
    )(embeddings, start_basis)
    return tuple(
        pl.pallas_call(
            functools.partial(small_kernel, row_factor),
            out_shape=[
                jax.ShapeDtypeStruct((cols, k), F32),
                jax.ShapeDtypeStruct((k, k), F32),
            ],
            in_specs=[vmem, vmem],
            out_specs=[vmem, vmem],
            scratch_shapes=[pltpu.VMEM((2, k, cols), F32), pltpu.VMEM((k, cols), F32)],
            compiler_params=pltpu.CompilerParams(vmem_limit_bytes=32 * 2**20),
            name="whiten",
        )(total, basis)
    )


def solution(mesh):
    placed = (P("dp", "col"), P("col", None))
    return jax.shard_map(
        on_device, mesh=mesh, in_specs=placed, out_specs=(P("col", None), P()), check_vma=False
    )
```

```python
import functools

import jax
import jax.numpy as jnp
from jax import lax
from jax.experimental import pallas as pl
from jax.experimental.pallas import tpu as pltpu
from jax.sharding import PartitionSpec as P

F32 = jnp.float32
BF16 = jnp.bfloat16
MESH = pl.DeviceIdType.MESH
CHUNK = 512
BLOCK = 512
LAG = 3
FLIGHT = 3
WIDTH, STEP = 32, 8
ORDER = (
    ("T", 1), ("T", 2), ("T", 3), ("G", 0), ("A", 0), ("A", 1), ("A", 2), ("G", 1), ("A", 3), ("B", 0),
    ("B", 1), ("G", 2), ("B", 2), ("H", 0), ("B", 3), ("E", 0), ("C", 0), ("C", 1), ("E", 1), ("C", 2),
    ("E", 2), ("C", 3), ("E", 3), ("W", 0), ("D", 0), ("S", 0), ("D", 1), ("S", 1), ("D", 2), ("S", 2),
    ("D", 3), ("S", 3),
)


STRIDES = (1, 4, 16)


def reduce_kernel(
    a_hbm, q_hbm, s_ref, gram_ref, factor_ref,
    a_v, q_v, p_own, p_other, img, t_own, t_sum, r1, r2, acc1,
    g_in, g_src, g_full, inv_v, fac_v, w_v, g2,
    load_sem, q_sem, ps_sem, pr_sem, s_sem, r_sem, gs_sem, gr_sem, hs_sem, hr_sem,
):
    rows, cols = a_v.shape
    n_chunk = rows // CHUNK
    n_block = cols // BLOCK
    dp = lax.axis_index("dp")
    core = lax.axis_index("col")

    def load(i):
        sl = pl.ds(pl.multiple_of(i * CHUNK, CHUNK), CHUNK)
        return pltpu.make_async_copy(a_hbm.at[sl], a_v.at[sl], load_sem.at[i])

    q_copy = pltpu.make_async_copy(q_hbm, q_v, q_sem)
    q_copy.start()
    for i in range(FLIGHT):
        load(i).start()

    sibling = {"dp": dp, "col": 1 - core}

    place = [lax.rem(lax.div(dp, stride), 4) for stride in STRIDES]
    onward = [[lax.rem(place[d] + offset, 4) for offset in range(4)] for d in range(3)]
    delta = [[(to - place[d]) * STRIDES[d] for to in onward[d]] for d in range(3)]

    def either(zero, one):
        return zero + core * (one - zero)

    orders = []
    for f in range(3):
        pair = [((f + s) % 3, (f + s + 1) % 3) for s in range(3)]
        orders.append((
            [either(place[d], place[e]) for d, e in pair],
            [[either(onward[d][o], onward[e][o]) for o in range(4)] for d, e in pair],
            [[either(delta[d][o], delta[e][o]) for o in range(4)] for d, e in pair],
        ))

    def device(shift):
        return {"dp": dp + shift, "col": core}

    barrier = pltpu.get_barrier_semaphore()
    pl.semaphore_signal(barrier, inc=1, device_id=sibling, device_id_type=MESH)
    shifts = [delta[d][o] for d in range(3) for o in range(1, 4)]
    shifts += [
        delta[d][o] + delta[(d + 1) % 3][u]
        for d in range(3) for o in range(1, 4) for u in range(1, 4)
    ]
    for shift in shifts:
        pl.semaphore_signal(barrier, inc=1, device_id=device(shift), device_id_type=MESH)

    def p_copy(i):
        sl = pl.ds(pl.multiple_of(i * CHUNK, CHUNK), CHUNK)
        return pltpu.make_async_remote_copy(
            src_ref=p_own.at[sl], dst_ref=p_other.at[sl],
            send_sem=ps_sem.at[i], recv_sem=pr_sem.at[i],
            device_id=sibling, device_id_type=MESH,
        )

    def multiply(i):
        sl = pl.ds(pl.multiple_of(i * CHUNK, CHUNK), CHUNK)
        p_own[sl] = jnp.dot(a_v[sl], q_v[...], preferred_element_type=F32)

    def combine(i):
        sl = pl.ds(pl.multiple_of(i * CHUNK, CHUNK), CHUNK)
        total = (p_own[sl] + p_other[sl]).T
        high = total.astype(BF16)
        img[0:128, sl] = high
        img[128:256, sl] = (total - high.astype(F32)).astype(BF16)

    q_copy.wait()
    for i in range(LAG):
        load(i).wait()
        load(i + FLIGHT).start()
        multiply(i)
    pl.semaphore_wait(barrier, 1 + len(shifts))
    for i in range(LAG):
        p_copy(i).start()

    def step(i, carry):
        load(i).wait()

        @pl.when(i + FLIGHT < n_chunk)
        def _():
            load(i + FLIGHT).start()

        p_copy(i - LAG).wait_recv()
        multiply(i)
        combine(i - LAG)
        p_copy(i).start()
        return carry

    lax.fori_loop(LAG, n_chunk, step, 0)
    for i in range(n_chunk - LAG, n_chunk - 1):
        p_copy(i).wait_recv()
        combine(i)

    def gram_send(stage, offset):
        here, _, shift = orders[0]
        return pltpu.make_async_remote_copy(
            src_ref=g_src.at[stage], dst_ref=g_in.at[stage, here[stage]],
            send_sem=gs_sem.at[stage, offset - 1], recv_sem=gr_sem.at[stage, offset - 1],
            device_id=device(shift[stage][offset]), device_id_type=MESH,
        )

    def gram_start(stage, value):
        g_src[stage] = value
        g_in[stage, orders[0][0][stage]] = value
        for offset in range(1, 4):
            gram_send(stage, offset).start()

    def gram_half():
        return pltpu.make_async_remote_copy(
            src_ref=g_full.at[core], dst_ref=g_full.at[core],
            send_sem=hs_sem.at[0], recv_sem=hr_sem.at[0],
            device_id=sibling, device_id_type=MESH,
        )

    def gram_advance(stage):
        for offset in range(1, 4):
            gram_send(stage, offset).wait_recv()
        value = (g_in[stage, 0] + g_in[stage, 1]) + (g_in[stage, 2] + g_in[stage, 3])
        if stage < 2:
            gram_start(stage + 1, value)
        else:
            g_full[core] = value
            gram_half().start()

    nt = (((1,), (1,)), ((), ()))
    early = rows - CHUNK

    def quad(rsl):
        part = img[:, rsl]
        both = lax.dot_general(part, part, nt, preferred_element_type=F32)
        return (both[0:128, 0:128] + both[128:256, 128:256]) + (
            both[0:128, 128:256] + both[128:256, 0:128]
        )

    def block(rsl, csl):
        both = jnp.dot(img[:, rsl], a_v[rsl, csl], preferred_element_type=F32)
        return both[0:128] + both[128:256]

    def send(b, stage, offset):
        here, there, shift = orders[2 * b % 3]
        c0 = b * BLOCK
        if stage in (0, 3):
            move = shift[0][offset]
            slot = 11 * stage + offset - 1
        else:
            o1, o2 = divmod(offset, 4)
            move = shift[1][o1] + shift[2][o2]
            slot = 3 + (stage - 1) * 15 + offset - 1
        if stage == 0:
            src = t_own.at[pl.ds(pl.multiple_of(there[0][offset] * 32, 32), 32), pl.ds(c0, BLOCK)]
            dst = r1.at[b, offset - 1]
        elif stage == 1:
            rsl = pl.ds(pl.multiple_of(there[1][o1] * 8, 8), 8)
            csl = pl.ds(pl.multiple_of(there[2][o2] * 128, 128), 128)
            src = acc1.at[b, rsl, csl]
            dst = r2.at[b, offset - 1]
        else:
            if stage == 2:
                rsl = pl.ds(pl.multiple_of(here[0] * 32 + here[1] * 8, 8), 8)
                csl = pl.ds(pl.multiple_of(c0 + here[2] * 128, 128), 128)
            else:
                rsl = pl.ds(pl.multiple_of(here[0] * 32, 32), 32)
                csl = pl.ds(c0, BLOCK)
            src = t_sum.at[rsl, csl]
            dst = t_sum.at[rsl, csl]
        return pltpu.make_async_remote_copy(
            src_ref=src, dst_ref=dst, send_sem=s_sem.at[b, slot], recv_sem=r_sem.at[b, slot],
            device_id=device(move), device_id_type=MESH,
        )

    def offsets(stage):
        return range(1, 4) if stage in (0, 3) else range(1, 16)

    def start(b, stage):
        for offset in offsets(stage):
            send(b, stage, offset).start()

    def advance(b, stage):
        here = orders[2 * b % 3][0]
        c0 = b * BLOCK
        for offset in offsets(stage):
            send(b, stage, offset).wait_recv()
        if stage == 0:
            own = t_own[pl.ds(pl.multiple_of(here[0] * 32, 32), 32), pl.ds(c0, BLOCK)]
            acc1[b] = (own + r1[b, 0]) + (r1[b, 1] + r1[b, 2])
        elif stage == 1:
            rsl = pl.ds(pl.multiple_of(here[1] * 8, 8), 8)
            csl = pl.ds(pl.multiple_of(here[2] * 128, 128), 128)
            parts = [acc1[b, rsl, csl]] + [r2[b, i] for i in range(15)]
            while len(parts) > 1:
                parts = [parts[i] + parts[i + 1] for i in range(0, len(parts), 2)]
            rsl = pl.ds(pl.multiple_of(here[0] * 32 + here[1] * 8, 8), 8)
            csl = pl.ds(pl.multiple_of(c0 + here[2] * 128, 128), 128)
            t_sum[rsl, csl] = parts[0]
        if stage < 3:
            start(b, stage + 1)

    t_own[:, 0:BLOCK] = block(pl.ds(0, early), pl.ds(0, BLOCK))
    inv_v[...] = quad(pl.ds(0, early))
    p_copy(n_chunk - 1).wait_recv()
    combine(n_chunk - 1)
    t_own[:, 0:BLOCK] += block(pl.ds(early, CHUNK), pl.ds(0, BLOCK))
    start(0, 0)
    inv_v[...] += quad(pl.ds(early, CHUNK))
    gram_start(0, inv_v[pl.ds(pl.multiple_of(core * 64, 64), 64)])

    for kind, n in ORDER:
        if kind == "T":
            csl = pl.ds(n * BLOCK, BLOCK)
            t_own[:, csl] = block(pl.ds(0, rows), csl)
            start(n, 0)
        elif kind == "G":
            gram_advance(n)
        elif kind == "H":
            gram_half().wait_recv()
            gram = g_full[...].reshape(128, 128)
            inv_v[...] = 0.5 * (gram + gram.T)
            fac_v[...] = jnp.zeros_like(fac_v)
        elif kind == "E":
            c0 = n * WIDTH
            done, rest, fac_v[c0:] = eliminate(inv_v[c0:], fac_v[c0:], c0, WIDTH, STEP)
            inv_v[c0 : c0 + WIDTH] = done
            if c0 + WIDTH < 128:
                inv_v[c0 + WIDTH :] = rest
        elif kind == "W":
            inv_v[...] = lower(inv_v[...])
            factor_ref[...] = fac_v[...]
            w_v[...] = fold3(
                lax.dot_general(split3(inv_v[...]), q_v[...], nt, preferred_element_type=F32)
            )
        elif kind == "S":
            csl = pl.ds(n * BLOCK, BLOCK)
            s_ref[:, csl] = jnp.dot(
                inv_v[...], t_sum[:, csl], precision=lax.Precision.HIGHEST,
                preferred_element_type=F32,
            )
            part = lax.dot_general(
                s_ref[:, csl], w_v[:, csl], nt, precision=lax.Precision.HIGHEST,
                preferred_element_type=F32,
            )
            g2[core] = part if n == 0 else g2[core] + part
        else:
            advance(n, "ABCD".index(kind))

    g2_copy = pltpu.make_async_remote_copy(
        src_ref=g2.at[core], dst_ref=g2.at[core], send_sem=hs_sem.at[1], recv_sem=hr_sem.at[1],
        device_id=sibling, device_id_type=MESH,
    )
    g2_copy.start()
    for i in range(n_chunk):
        p_copy(i).wait_send()
    for b in range(n_block):
        for stage in range(4):
            for offset in offsets(stage):
                send(b, stage, offset).wait_send()
    for stage in range(3):
        for offset in range(1, 4):
            gram_send(stage, offset).wait_send()
    gram_half().wait_send()
    g2_copy.wait()
    gram_ref[...] = g2[0] + g2[1]


def eliminate(rest, factor, c0, width, step):
    size = rest.shape[1]
    done = []
    for start in range(c0, c0 + width, step):
        n = rest.shape[0]
        lane = lax.broadcasted_iota(jnp.int32, (n, size), 1)
        row = lax.broadcasted_iota(jnp.int32, (n, size), 0)
        cols = [jnp.broadcast_to(rest[:, start + k : start + k + 1], (n, size)) for k in range(step)]
        eye = jnp.where(lane == row + start, 1.0, 0.0).astype(F32)
        rest = jnp.where((lane >= start) & (lane < start + step), eye, rest)
        scale = jnp.zeros((step, size), F32)
        part = jnp.zeros((n, size), F32)
        for k in range(step):
            pivot = cols[k][k : k + 1]
            root = lax.rsqrt(pivot)
            scale = jnp.where(row[:step] == k, root, scale)
            if factor is not None:
                part = jnp.where((lane == start + k) & (row >= k), cols[k] * root, part)
            mult = jnp.where(row > k, cols[k] * (1.0 / pivot), 0.0)
            for later in range(k + 1, step):
                cols[later] = cols[later] - mult * cols[later][k : k + 1]
            rest = rest - mult * rest[k : k + 1]
        if factor is not None:
            ahead = factor.shape[0] - n
            factor = factor + part if not ahead else jnp.concatenate(
                [factor[:ahead], factor[ahead:] + part], 0
            )
        done.append(rest[:step] * scale)
        rest = rest[step:]
    return jnp.concatenate(done, 0), rest, factor


def split3(x):
    high = x.astype(BF16)
    rest = x - high.astype(F32)
    mid = rest.astype(BF16)
    low = (rest - mid.astype(F32)).astype(BF16)
    return jnp.concatenate([high, mid, low], 0)


def fold3(x):
    n = x.shape[0] // 3
    return x[0:n] + (x[n : 2 * n] + x[2 * n :])


def lower(x):
    lane = lax.broadcasted_iota(jnp.int32, x.shape, 1)
    row = lax.broadcasted_iota(jnp.int32, x.shape, 0)
    return jnp.where(lane <= row, x, 0.0)


def final_kernel(row_factor, s_ref, gram_ref, factor_ref, out_ref, scaled_ref):
    scaled_ref[...] = factor_ref[...] * row_factor
    gram = gram_ref[...]
    inverse, _, _ = eliminate(0.5 * (gram + gram.T), None, 0, gram.shape[0], STEP)
    inverse = lower(inverse) * row_factor
    final = jnp.dot(
        inverse, s_ref[...], precision=lax.Precision.HIGHEST, preferred_element_type=F32
    )
    out_ref[...] = final.T


def on_device(embeddings, start_basis):
    rows, cols = embeddings.shape
    k = start_basis.shape[1]
    n_block = cols // BLOCK
    n_chunk = rows // CHUNK
    row_factor = (rows * lax.axis_size("dp")) ** (-0.5)
    vmem = pl.BlockSpec(memory_space=pltpu.VMEM)
    anywhere = pl.BlockSpec(memory_space=pltpu.HBM)
    dma = pltpu.SemaphoreType.DMA
    whitened, gram, factor = pl.pallas_call(
        reduce_kernel,
        out_shape=[
            jax.ShapeDtypeStruct((k, cols), F32),
            jax.ShapeDtypeStruct((k, k), F32),
            jax.ShapeDtypeStruct((k, k), F32),
        ],
        in_specs=[anywhere, anywhere],
        out_specs=[vmem, vmem, vmem],
        scratch_shapes=[
            pltpu.VMEM((rows, cols), BF16),
            pltpu.VMEM((cols, k), BF16),
            pltpu.VMEM((rows, k), F32),
            pltpu.VMEM((rows, k), F32),
            pltpu.VMEM((2 * k, rows), BF16),
            pltpu.VMEM((k, cols), F32),
            pltpu.VMEM((k, cols), F32),
            pltpu.VMEM((n_block, 3, 32, BLOCK), F32),
            pltpu.VMEM((n_block, 15, 8, 128), F32),
            pltpu.VMEM((n_block, 32, BLOCK), F32),
            pltpu.VMEM((3, 4, k // 2, k), F32),
            pltpu.VMEM((3, k // 2, k), F32),
            pltpu.VMEM((2, k // 2, k), F32),
            pltpu.VMEM((k, k), F32),
            pltpu.VMEM((k, k), F32),
            pltpu.VMEM((k, cols), F32),
            pltpu.VMEM((2, k, k), F32),
            dma((n_chunk,)), dma, dma((n_chunk,)), dma((n_chunk,)),
            dma((n_block, 36)), dma((n_block, 36)),
            dma((3, 3)), dma((3, 3)), dma((2,)), dma((2,)),
        ],
        compiler_params=pltpu.CompilerParams(
            collective_id=0, has_side_effects=True, vmem_limit_bytes=52 * 2**20
        ),
        name="image_and_sum",
    )(embeddings, start_basis)
    return tuple(
        pl.pallas_call(
            functools.partial(final_kernel, row_factor),
            out_shape=[
                jax.ShapeDtypeStruct((cols, k), F32),
                jax.ShapeDtypeStruct((k, k), F32),
            ],
            in_specs=[vmem, vmem, vmem],
            out_specs=[vmem, vmem],
            compiler_params=pltpu.CompilerParams(vmem_limit_bytes=32 * 2**20),
            name="final",
        )(whitened, gram, factor)
    )


def solution(mesh):
    placed = (P("dp", "col"), P("col", None))
    return jax.shard_map(
        on_device, mesh=mesh, in_specs=placed, out_specs=(P("col", None), P()), check_vma=False
    )
```

```python
import functools

import jax
import jax.numpy as jnp
from jax import lax
from jax.experimental import pallas as pl
from jax.experimental.pallas import tpu as pltpu
from jax.sharding import PartitionSpec as P

F32 = jnp.float32
BF16 = jnp.bfloat16
MESH = pl.DeviceIdType.MESH
CHUNK = 512
BLOCK = 512
LAG = 3
FLIGHT = 3
WIDTH, STEP = 32, 8
ORDER = (("T", 1), ("T", 2), ("T", 3), ("G", 0), ("A", 0), ("A", 1), ("A", 2), ("G", 1), ("A", 3), ("B", 0), ("B", 1), ("G", 2), ("B", 2), ("H", 0), ("B", 3), ("E", 0), ("C", 0), ("C", 1), ("E", 1), ("C", 2), ("E", 2), ("C", 3), ("E", 3), ("W", 0), ("D", 0), ("S", 0), ("D", 1), ("S", 1), ("D", 2), ("S", 2), ("D", 3), ("S", 3), )


STRIDES = (1, 4, 16)


def reduce_kernel(
    a_hbm, q_hbm, s_ref, gram_ref, factor_ref,
    a_v, q_v, p_own, p_other, img, t_own, t_sum, r1, r2, acc1,
    g_in, g_src, g_full, inv_v, fac_v, w_v, g2,
    load_sem, q_sem, ps_sem, pr_sem, s_sem, r_sem, gs_sem, gr_sem, hs_sem, hr_sem,
):
    rows, cols = a_v.shape
    n_chunk = rows // CHUNK
    n_block = cols // BLOCK
    dp = lax.axis_index("dp")
    core = lax.axis_index("col")

    def load(i):
        sl = pl.ds(pl.multiple_of(i * CHUNK, CHUNK), CHUNK)
        return pltpu.make_async_copy(a_hbm.at[sl], a_v.at[sl], load_sem.at[i])

    q_copy = pltpu.make_async_copy(q_hbm, q_v, q_sem)
    q_copy.start()
    load(0).start()

    sibling = {"dp": dp, "col": 1 - core}

    place = [lax.rem(lax.div(dp, stride), 4) for stride in STRIDES]
    onward = [[lax.rem(place[d] + offset, 4) for offset in range(4)] for d in range(3)]
    delta = [[(to - place[d]) * STRIDES[d] for to in onward[d]] for d in range(3)]

    def either(zero, one):
        return zero + core * (one - zero)

    orders = []
    for f in range(3):
        pair = [((f + s) % 3, (f + s + 1) % 3) for s in range(3)]
        orders.append((
            [either(place[d], place[e]) for d, e in pair],
            [[either(onward[d][o], onward[e][o]) for o in range(4)] for d, e in pair],
            [[either(delta[d][o], delta[e][o]) for o in range(4)] for d, e in pair],
        ))

    def device(shift):
        return {"dp": dp + shift, "col": core}

    barrier = pltpu.get_barrier_semaphore()
    pl.semaphore_signal(barrier, inc=1, device_id=sibling, device_id_type=MESH)
    shifts = [delta[d][o] for d in range(3) for o in range(1, 4)]
    shifts += [
        delta[d][o] + delta[(d + 1) % 3][u]
        for d in range(3) for o in range(1, 4) for u in range(1, 4)
    ]
    for shift in shifts:
        pl.semaphore_signal(barrier, inc=1, device_id=device(shift), device_id_type=MESH)

    def p_copy(i):
        sl = pl.ds(pl.multiple_of(i * CHUNK, CHUNK), CHUNK)
        return pltpu.make_async_remote_copy(
            src_ref=p_own.at[sl], dst_ref=p_other.at[sl],
            send_sem=ps_sem.at[i], recv_sem=pr_sem.at[i],
            device_id=sibling, device_id_type=MESH,
        )

    def multiply(i):
        sl = pl.ds(pl.multiple_of(i * CHUNK, CHUNK), CHUNK)
        p_own[sl] = jnp.dot(a_v[sl], q_v[...], preferred_element_type=F32)

    def combine(i):
        sl = pl.ds(pl.multiple_of(i * CHUNK, CHUNK), CHUNK)
        total = (p_own[sl] + p_other[sl]).T
        high = total.astype(BF16)
        img[0:128, sl] = high
        img[128:256, sl] = (total - high.astype(F32)).astype(BF16)

    for i in range(1, FLIGHT):
        load(i).start()
    q_copy.wait()
    for i in range(LAG):
        load(i).wait()
        load(i + FLIGHT).start()
        multiply(i)
    pl.semaphore_wait(barrier, 1 + len(shifts))
    for i in range(LAG):
        p_copy(i).start()

    def step(i, carry):
        load(i).wait()

        @pl.when(i + FLIGHT < n_chunk)
        def _():
            load(i + FLIGHT).start()

        p_copy(i - LAG).wait_recv()
        multiply(i)
        combine(i - LAG)
        p_copy(i).start()
        return carry

    lax.fori_loop(LAG, n_chunk, step, 0)
    for i in range(n_chunk - LAG, n_chunk - 1):
        p_copy(i).wait_recv()
        combine(i)

    def gram_send(stage, offset):
        here, _, shift = orders[0]
        return pltpu.make_async_remote_copy(
            src_ref=g_src.at[stage], dst_ref=g_in.at[stage, here[stage]],
            send_sem=gs_sem.at[stage, offset - 1], recv_sem=gr_sem.at[stage, offset - 1],
            device_id=device(shift[stage][offset]), device_id_type=MESH,
        )

    def gram_start(stage, value):
        g_src[stage] = value
        g_in[stage, orders[0][0][stage]] = value
        for offset in range(1, 4):
            gram_send(stage, offset).start()

    def gram_half():
        return pltpu.make_async_remote_copy(
            src_ref=g_full.at[core], dst_ref=g_full.at[core],
            send_sem=hs_sem.at[0], recv_sem=hr_sem.at[0],
            device_id=sibling, device_id_type=MESH,
        )

    def gram_advance(stage):
        for offset in range(1, 4):
            gram_send(stage, offset).wait_recv()
        value = (g_in[stage, 0] + g_in[stage, 1]) + (g_in[stage, 2] + g_in[stage, 3])
        if stage < 2:
            gram_start(stage + 1, value)
        else:
            g_full[core] = value
            gram_half().start()

    nt = (((1,), (1,)), ((), ()))
    early = rows - CHUNK

    def quad(rsl):
        part = img[:, rsl]
        both = lax.dot_general(part, part, nt, preferred_element_type=F32)
        return (both[0:128, 0:128] + both[128:256, 128:256]) + (
            both[0:128, 128:256] + both[128:256, 0:128]
        )

    def block(rsl, csl):
        both = jnp.dot(img[:, rsl], a_v[rsl, csl], preferred_element_type=F32)
        return both[0:128] + both[128:256]

    def send(b, stage, offset):
        here, there, shift = orders[2 * b % 3]
        c0 = b * BLOCK
        if stage in (0, 3):
            move = shift[0][offset]
            slot = 11 * stage + offset - 1
        else:
            o1, o2 = divmod(offset, 4)
            move = shift[1][o1] + shift[2][o2]
            slot = 3 + (stage - 1) * 15 + offset - 1
        if stage == 0:
            src = t_own.at[pl.ds(pl.multiple_of(there[0][offset] * 32, 32), 32), pl.ds(c0, BLOCK)]
            dst = r1.at[b, offset - 1]
        elif stage == 1:
            rsl = pl.ds(pl.multiple_of(there[1][o1] * 8, 8), 8)
            csl = pl.ds(pl.multiple_of(there[2][o2] * 128, 128), 128)
            src = acc1.at[b, rsl, csl]
            dst = r2.at[b, offset - 1]
        else:
            if stage == 2:
                rsl = pl.ds(pl.multiple_of(here[0] * 32 + here[1] * 8, 8), 8)
                csl = pl.ds(pl.multiple_of(c0 + here[2] * 128, 128), 128)
            else:
                rsl = pl.ds(pl.multiple_of(here[0] * 32, 32), 32)
                csl = pl.ds(c0, BLOCK)
            src = t_sum.at[rsl, csl]
            dst = t_sum.at[rsl, csl]
        return pltpu.make_async_remote_copy(
            src_ref=src, dst_ref=dst, send_sem=s_sem.at[b, slot], recv_sem=r_sem.at[b, slot],
            device_id=device(move), device_id_type=MESH,
        )

    def offsets(stage):
        return range(1, 4) if stage in (0, 3) else range(1, 16)

    def start(b, stage):
        for offset in offsets(stage):
            send(b, stage, offset).start()

    def advance(b, stage):
        here = orders[2 * b % 3][0]
        c0 = b * BLOCK
        for offset in offsets(stage):
            send(b, stage, offset).wait_recv()
        if stage == 0:
            own = t_own[pl.ds(pl.multiple_of(here[0] * 32, 32), 32), pl.ds(c0, BLOCK)]
            acc1[b] = (own + r1[b, 0]) + (r1[b, 1] + r1[b, 2])
        elif stage == 1:
            rsl = pl.ds(pl.multiple_of(here[1] * 8, 8), 8)
            csl = pl.ds(pl.multiple_of(here[2] * 128, 128), 128)
            parts = [acc1[b, rsl, csl]] + [r2[b, i] for i in range(15)]
            while len(parts) > 1:
                parts = [parts[i] + parts[i + 1] for i in range(0, len(parts), 2)]
            rsl = pl.ds(pl.multiple_of(here[0] * 32 + here[1] * 8, 8), 8)
            csl = pl.ds(pl.multiple_of(c0 + here[2] * 128, 128), 128)
            t_sum[rsl, csl] = parts[0]
        if stage < 3:
            start(b, stage + 1)

    t_own[:, 0:BLOCK] = block(pl.ds(0, early), pl.ds(0, BLOCK))
    inv_v[...] = quad(pl.ds(0, early))
    p_copy(n_chunk - 1).wait_recv()
    combine(n_chunk - 1)
    t_own[:, 0:BLOCK] += block(pl.ds(early, CHUNK), pl.ds(0, BLOCK))
    start(0, 0)
    inv_v[...] += quad(pl.ds(early, CHUNK))
    gram_start(0, inv_v[pl.ds(pl.multiple_of(core * 64, 64), 64)])

    for kind, n in ORDER:
        if kind == "T":
            csl = pl.ds(n * BLOCK, BLOCK)
            t_own[:, csl] = block(pl.ds(0, rows), csl)
            start(n, 0)
        elif kind == "G":
            gram_advance(n)
        elif kind == "H":
            gram_half().wait_recv()
            gram = g_full[...].reshape(128, 128)
            inv_v[...] = 0.5 * (gram + gram.T)
            fac_v[...] = jnp.zeros_like(fac_v)
        elif kind == "E":
            c0 = n * WIDTH
            done, rest, fac_v[c0:] = eliminate(inv_v[c0:], fac_v[c0:], c0, WIDTH, STEP)
            inv_v[c0 : c0 + WIDTH] = done
            if c0 + WIDTH < 128:
                inv_v[c0 + WIDTH :] = rest
        elif kind == "W":
            inv_v[...] = lower(inv_v[...])
            factor_ref[...] = fac_v[...]
            w_v[...] = fold3(
                lax.dot_general(split3(inv_v[...]), q_v[...], nt, preferred_element_type=F32)
            )
        elif kind == "S":
            csl = pl.ds(n * BLOCK, BLOCK)
            s_ref[:, csl] = jnp.dot(
                inv_v[...], t_sum[:, csl], precision=lax.Precision.HIGHEST,
                preferred_element_type=F32,
            )
            part = lax.dot_general(
                s_ref[:, csl], w_v[:, csl], nt, precision=lax.Precision.HIGHEST,
                preferred_element_type=F32,
            )
            g2[core] = part if n == 0 else g2[core] + part
        else:
            advance(n, "ABCD".index(kind))

    g2_copy = pltpu.make_async_remote_copy(
        src_ref=g2.at[core], dst_ref=g2.at[core], send_sem=hs_sem.at[1], recv_sem=hr_sem.at[1],
        device_id=sibling, device_id_type=MESH,
    )
    g2_copy.start()
    for i in range(n_chunk):
        p_copy(i).wait_send()
    for b in range(n_block):
        for stage in range(4):
            for offset in offsets(stage):
                send(b, stage, offset).wait_send()
    for stage in range(3):
        for offset in range(1, 4):
            gram_send(stage, offset).wait_send()
    gram_half().wait_send()
    g2_copy.wait()
    gram_ref[...] = g2[0] + g2[1]


def eliminate(rest, factor, c0, width, step):
    size = rest.shape[1]
    done = []
    for start in range(c0, c0 + width, step):
        n = rest.shape[0]
        lane = lax.broadcasted_iota(jnp.int32, (n, size), 1)
        row = lax.broadcasted_iota(jnp.int32, (n, size), 0)
        cols = [jnp.broadcast_to(rest[:, start + k : start + k + 1], (n, size)) for k in range(step)]
        eye = jnp.where(lane == row + start, 1.0, 0.0).astype(F32)
        rest = jnp.where((lane >= start) & (lane < start + step), eye, rest)
        scale = jnp.zeros((step, size), F32)
        part = jnp.zeros((n, size), F32)
        for k in range(step):
            pivot = cols[k][k : k + 1]
            root = lax.rsqrt(pivot)
            scale = jnp.where(row[:step] == k, root, scale)
            if factor is not None:
                part = jnp.where((lane == start + k) & (row >= k), cols[k] * root, part)
            mult = jnp.where(row > k, cols[k] * (1.0 / pivot), 0.0)
            for later in range(k + 1, step):
                cols[later] = cols[later] - mult * cols[later][k : k + 1]
            rest = rest - mult * rest[k : k + 1]
        if factor is not None:
            ahead = factor.shape[0] - n
            factor = factor + part if not ahead else jnp.concatenate(
                [factor[:ahead], factor[ahead:] + part], 0
            )
        done.append(rest[:step] * scale)
        rest = rest[step:]
    return jnp.concatenate(done, 0), rest, factor


def terms3(x):
    high = x.astype(BF16)
    rest = x - high.astype(F32)
    mid = rest.astype(BF16)
    return high, mid, (rest - mid.astype(F32)).astype(BF16)


def split3(x):
    return jnp.concatenate(terms3(x), 0)


def fold3(x):
    n = x.shape[0] // 3
    return x[0:n] + (x[n : 2 * n] + x[2 * n :])


def inverse_by_blocks(rest, step):
    size = rest.shape[0]
    lane = lax.broadcasted_iota(jnp.int32, (size, size), 1)
    row = lax.broadcasted_iota(jnp.int32, (step, size), 0)
    done = []
    for start in range(0, size, step):
        n = size - start
        block = (lane >= start) & (lane < start + step)

        def column(k, rows):
            return jnp.broadcast_to(rows[:, start + k : start + k + 1], rows.shape)

        cols = [column(k, rest[:step]) for k in range(step)]
        eye = jnp.where(lane[:step] == row + start, 1.0, 0.0).astype(F32)
        down = jnp.where(block[:step], eye, rest[:step])
        full = down
        pivots = []
        for k in range(step):
            pivots.append(cols[k][k : k + 1])
            mult = cols[k] * (1.0 / pivots[k])
            below = jnp.where(row > k, mult, 0.0)
            others = jnp.where(row != k, mult, 0.0)
            for later in range(k + 1, step):
                cols[later] = cols[later] - others * cols[later][k : k + 1]
            line = down[k : k + 1]
            down = down - below * line
            full = full - others * line
        pivots = jnp.concatenate(pivots, 0)
        done.append(down * lax.rsqrt(pivots))
        if n > step:
            full = full * (1.0 / pivots)
            terms = [column(k, rest[step:]) * full[k : k + 1] for k in range(step)]
            while len(terms) > 1:
                terms = [terms[i] + terms[i + 1] for i in range(0, len(terms), 2)]
            rest = jnp.where(block[: n - step], 0.0, rest[step:]) - terms[0]
    return lower(jnp.concatenate(done, 0))


def lower(x):
    lane = lax.broadcasted_iota(jnp.int32, x.shape, 1)
    row = lax.broadcasted_iota(jnp.int32, x.shape, 0)
    return jnp.where(lane <= row, x, 0.0)


def final_kernel(row_factor, s_ref, gram_ref, factor_ref, out_ref, scaled_ref, right_v):
    scaled_ref[...] = factor_ref[...] * row_factor
    high, mid, low = terms3(s_ref[...])
    for place, term in enumerate((high, mid, high, mid, low, high)):
        right_v[128 * place : 128 * (place + 1)] = term
    gram = gram_ref[...]
    inverse = inverse_by_blocks(0.5 * (gram + gram.T), 2 * STEP) * row_factor
    high, mid, low = terms3(inverse)
    left = jnp.concatenate([high, high, mid, mid, high, low], 1)
    out_ref[...] = jnp.dot(left, right_v[...], preferred_element_type=F32).T


def on_device(embeddings, start_basis):
    rows, cols = embeddings.shape
    k = start_basis.shape[1]
    n_block = cols // BLOCK
    n_chunk = rows // CHUNK
    row_factor = (rows * lax.axis_size("dp")) ** (-0.5)
    vmem = pl.BlockSpec(memory_space=pltpu.VMEM)
    anywhere = pl.BlockSpec(memory_space=pltpu.HBM)
    dma = pltpu.SemaphoreType.DMA
    whitened, gram, factor = pl.pallas_call(
        reduce_kernel,
        out_shape=[
            jax.ShapeDtypeStruct((k, cols), F32),
            jax.ShapeDtypeStruct((k, k), F32),
            jax.ShapeDtypeStruct((k, k), F32),
        ],
        in_specs=[anywhere, anywhere],
        out_specs=[vmem, vmem, vmem],
        scratch_shapes=[
            pltpu.VMEM((rows, cols), BF16),
            pltpu.VMEM((cols, k), BF16),
            pltpu.VMEM((rows, k), F32),
            pltpu.VMEM((rows, k), F32),
            pltpu.VMEM((2 * k, rows), BF16),
            pltpu.VMEM((k, cols), F32),
            pltpu.VMEM((k, cols), F32),
            pltpu.VMEM((n_block, 3, 32, BLOCK), F32),
            pltpu.VMEM((n_block, 15, 8, 128), F32),
            pltpu.VMEM((n_block, 32, BLOCK), F32),
            pltpu.VMEM((3, 4, k // 2, k), F32),
            pltpu.VMEM((3, k // 2, k), F32),
            pltpu.VMEM((2, k // 2, k), F32),
            pltpu.VMEM((k, k), F32),
            pltpu.VMEM((k, k), F32),
            pltpu.VMEM((k, cols), F32),
            pltpu.VMEM((2, k, k), F32),
            dma((n_chunk,)), dma, dma((n_chunk,)), dma((n_chunk,)),
            dma((n_block, 36)), dma((n_block, 36)),
            dma((3, 3)), dma((3, 3)), dma((2,)), dma((2,)),
        ],
        compiler_params=pltpu.CompilerParams(
            collective_id=0, has_side_effects=True, vmem_limit_bytes=52 * 2**20
        ),
        name="image_and_sum",
    )(embeddings, pltpu.with_memory_space_constraint(start_basis, pltpu.HBM))
    return tuple(
        pl.pallas_call(
            functools.partial(final_kernel, row_factor),
            out_shape=[
                jax.ShapeDtypeStruct((cols, k), F32),
                jax.ShapeDtypeStruct((k, k), F32),
            ],
            in_specs=[vmem, vmem, vmem],
            out_specs=[vmem, vmem],
            scratch_shapes=[pltpu.VMEM((6 * k, cols), BF16)],
            compiler_params=pltpu.CompilerParams(vmem_limit_bytes=32 * 2**20),
            name="final",
        )(whitened, gram, factor)
    )


def solution(mesh):
    placed = (P("dp", "col"), P("col", None))
    return jax.shard_map(
        on_device, mesh=mesh, in_specs=placed, out_specs=(P("col", None), P()), check_vma=False
    )
```

```python
import functools

import jax
import jax.numpy as jnp
from jax import lax
from jax.experimental import pallas as pl
from jax.experimental.pallas import tpu as pltpu
from jax.sharding import PartitionSpec as P

F32 = jnp.float32
BF16 = jnp.bfloat16
MESH = pl.DeviceIdType.MESH
CHUNK = 512
BLOCK = 512
LAG = 3
FLIGHT = 3
WIDTH, STEP = 32, 8
ORDER = (
    ("T", 1), ("T", 2), ("T", 3), ("A", 0), ("G", 0), ("A", 1), ("A", 2), ("A", 3), ("G", 1), ("B", 0),
    ("B", 1), ("B", 2), ("G", 2), ("B", 3), ("H", 0), ("E", 0), ("C", 0), ("C", 1), ("E", 1), ("C", 2),
    ("E", 2), ("C", 3), ("E", 3), ("W", 0), ("D", 0), ("S", 0), ("D", 1), ("S", 1), ("D", 2), ("S", 2),
    ("D", 3), ("S", 3),
)


STRIDES = (1, 4, 16)


def reduce_kernel(
    a_hbm, q_hbm, s_ref, gram_ref, factor_ref,
    a_v, q_v, p_own, p_other, img, t_own, t_sum, r1, r2, acc1,
    g_in, g_src, g_full, inv_v, fac_v, w_v, g2,
    load_sem, q_sem, ps_sem, pr_sem, s_sem, r_sem, gs_sem, gr_sem, hs_sem, hr_sem,
):
    rows, cols = a_v.shape
    n_chunk = rows // CHUNK
    n_block = cols // BLOCK
    dp = lax.axis_index("dp")
    core = lax.axis_index("col")

    def load(i):
        sl = pl.ds(pl.multiple_of(i * CHUNK, CHUNK), CHUNK)
        return pltpu.make_async_copy(a_hbm.at[sl], a_v.at[sl], load_sem.at[i])

    q_copy = pltpu.make_async_copy(q_hbm, q_v, q_sem)
    q_copy.start()
    load(0).start()

    sibling = {"dp": dp, "col": 1 - core}

    place = [lax.rem(lax.div(dp, stride), 4) for stride in STRIDES]
    onward = [[lax.rem(place[d] + offset, 4) for offset in range(4)] for d in range(3)]
    delta = [[(to - place[d]) * STRIDES[d] for to in onward[d]] for d in range(3)]

    def either(zero, one):
        return zero + core * (one - zero)

    orders = []
    for f in range(3):
        pair = [((f + s) % 3, (f + s + 1) % 3) for s in range(3)]
        orders.append((
            [either(place[d], place[e]) for d, e in pair],
            [[either(onward[d][o], onward[e][o]) for o in range(4)] for d, e in pair],
            [[either(delta[d][o], delta[e][o]) for o in range(4)] for d, e in pair],
        ))

    def device(shift):
        return {"dp": dp + shift, "col": core}

    barrier = pltpu.get_barrier_semaphore()
    pl.semaphore_signal(barrier, inc=1, device_id=sibling, device_id_type=MESH)
    shifts = [delta[d][o] for d in range(3) for o in range(1, 4)]
    shifts += [
        delta[d][o] + delta[(d + 1) % 3][u]
        for d in range(3) for o in range(1, 4) for u in range(1, 4)
    ]
    for shift in shifts:
        pl.semaphore_signal(barrier, inc=1, device_id=device(shift), device_id_type=MESH)

    def p_copy(i):
        sl = pl.ds(pl.multiple_of(i * CHUNK, CHUNK), CHUNK)
        return pltpu.make_async_remote_copy(
            src_ref=p_own.at[sl], dst_ref=p_other.at[sl],
            send_sem=ps_sem.at[i], recv_sem=pr_sem.at[i],
            device_id=sibling, device_id_type=MESH,
        )

    def multiply(i):
        sl = pl.ds(pl.multiple_of(i * CHUNK, CHUNK), CHUNK)
        p_own[sl] = jnp.dot(a_v[sl], q_v[...], preferred_element_type=F32)

    def combine(i):
        sl = pl.ds(pl.multiple_of(i * CHUNK, CHUNK), CHUNK)
        total = (p_own[sl] + p_other[sl]).T
        high = total.astype(BF16)
        img[0:128, sl] = high
        img[128:256, sl] = (total - high.astype(F32)).astype(BF16)

    for i in range(1, FLIGHT):
        load(i).start()
    q_copy.wait()
    for i in range(LAG):
        load(i).wait()
        load(i + FLIGHT).start()
        multiply(i)
    pl.semaphore_wait(barrier, 1 + len(shifts))
    for i in range(LAG):
        p_copy(i).start()

    def step(i, carry):
        load(i).wait()

        @pl.when(i + FLIGHT < n_chunk)
        def _():
            load(i + FLIGHT).start()

        p_copy(i - LAG).wait_recv()
        multiply(i)
        combine(i - LAG)
        p_copy(i).start()
        return carry

    lax.fori_loop(LAG, n_chunk, step, 0)
    for i in range(n_chunk - LAG, n_chunk - 1):
        p_copy(i).wait_recv()
        combine(i)

    def gram_send(stage, offset):
        here, _, shift = orders[0]
        return pltpu.make_async_remote_copy(
            src_ref=g_src.at[stage], dst_ref=g_in.at[stage, here[stage]],
            send_sem=gs_sem.at[stage, offset - 1], recv_sem=gr_sem.at[stage, offset - 1],
            device_id=device(shift[stage][offset]), device_id_type=MESH,
        )

    def gram_start(stage, value):
        g_src[stage] = value
        g_in[stage, orders[0][0][stage]] = value
        for offset in range(1, 4):
            gram_send(stage, offset).start()

    def gram_half():
        return pltpu.make_async_remote_copy(
            src_ref=g_full.at[core], dst_ref=g_full.at[core],
            send_sem=hs_sem.at[0], recv_sem=hr_sem.at[0],
            device_id=sibling, device_id_type=MESH,
        )

    def gram_advance(stage):
        for offset in range(1, 4):
            gram_send(stage, offset).wait_recv()
        value = (g_in[stage, 0] + g_in[stage, 1]) + (g_in[stage, 2] + g_in[stage, 3])
        if stage < 2:
            gram_start(stage + 1, value)
        else:
            g_full[core] = value
            gram_half().start()

    nt = (((1,), (1,)), ((), ()))
    early = rows - CHUNK

    def quad(rsl):
        part = img[:, rsl]
        both = lax.dot_general(part, part, nt, preferred_element_type=F32)
        return (both[0:128, 0:128] + both[128:256, 128:256]) + (
            both[0:128, 128:256] + both[128:256, 0:128]
        )

    def block(rsl, csl):
        both = jnp.dot(img[:, rsl], a_v[rsl, csl], preferred_element_type=F32)
        return both[0:128] + both[128:256]

    def send(b, stage, offset):
        here, there, shift = orders[2 * b % 3]
        c0 = b * BLOCK
        if stage in (0, 3):
            move = shift[0][offset]
            slot = 11 * stage + offset - 1
        else:
            o1, o2 = divmod(offset, 4)
            move = shift[1][o1] + shift[2][o2]
            slot = 3 + (stage - 1) * 15 + offset - 1
        if stage == 0:
            src = t_own.at[pl.ds(pl.multiple_of(there[0][offset] * 32, 32), 32), pl.ds(c0, BLOCK)]
            dst = r1.at[b, offset - 1]
        elif stage == 1:
            rsl = pl.ds(pl.multiple_of(there[1][o1] * 8, 8), 8)
            csl = pl.ds(pl.multiple_of(there[2][o2] * 128, 128), 128)
            src = acc1.at[b, rsl, csl]
            dst = r2.at[b, offset - 1]
        else:
            if stage == 2:
                rsl = pl.ds(pl.multiple_of(here[0] * 32 + here[1] * 8, 8), 8)
                csl = pl.ds(pl.multiple_of(c0 + here[2] * 128, 128), 128)
            else:
                rsl = pl.ds(pl.multiple_of(here[0] * 32, 32), 32)
                csl = pl.ds(c0, BLOCK)
            src = t_sum.at[rsl, csl]
            dst = t_sum.at[rsl, csl]
        return pltpu.make_async_remote_copy(
            src_ref=src, dst_ref=dst, send_sem=s_sem.at[b, slot], recv_sem=r_sem.at[b, slot],
            device_id=device(move), device_id_type=MESH,
        )

    def offsets(stage):
        return range(1, 4) if stage in (0, 3) else range(1, 16)

    def start(b, stage):
        for offset in offsets(stage):
            send(b, stage, offset).start()

    def advance(b, stage):
        here = orders[2 * b % 3][0]
        c0 = b * BLOCK
        for offset in offsets(stage):
            send(b, stage, offset).wait_recv()
        if stage == 0:
            own = t_own[pl.ds(pl.multiple_of(here[0] * 32, 32), 32), pl.ds(c0, BLOCK)]
            acc1[b] = (own + r1[b, 0]) + (r1[b, 1] + r1[b, 2])
        elif stage == 1:
            rsl = pl.ds(pl.multiple_of(here[1] * 8, 8), 8)
            csl = pl.ds(pl.multiple_of(here[2] * 128, 128), 128)
            parts = [acc1[b, rsl, csl]] + [r2[b, i] for i in range(15)]
            while len(parts) > 1:
                parts = [parts[i] + parts[i + 1] for i in range(0, len(parts), 2)]
            rsl = pl.ds(pl.multiple_of(here[0] * 32 + here[1] * 8, 8), 8)
            csl = pl.ds(pl.multiple_of(c0 + here[2] * 128, 128), 128)
            t_sum[rsl, csl] = parts[0]
        if stage < 3:
            start(b, stage + 1)

    t_own[:, 0:BLOCK] = block(pl.ds(0, early), pl.ds(0, BLOCK))
    inv_v[...] = quad(pl.ds(0, early))
    p_copy(n_chunk - 1).wait_recv()
    combine(n_chunk - 1)
    t_own[:, 0:BLOCK] += block(pl.ds(early, CHUNK), pl.ds(0, BLOCK))
    start(0, 0)
    inv_v[...] += quad(pl.ds(early, CHUNK))
    gram_start(0, inv_v[pl.ds(pl.multiple_of(core * 64, 64), 64)])

    for kind, n in ORDER:
        if kind == "T":
            csl = pl.ds(n * BLOCK, BLOCK)
            t_own[:, csl] = block(pl.ds(0, rows), csl)
            start(n, 0)
        elif kind == "G":
            gram_advance(n)
        elif kind == "H":
            gram_half().wait_recv()
            gram = g_full[...].reshape(128, 128)
            inv_v[...] = 0.5 * (gram + gram.T)
            fac_v[...] = jnp.zeros_like(fac_v)
        elif kind == "E":
            c0 = n * WIDTH
            done, rest, fac_v[c0:] = eliminate(inv_v[c0:], fac_v[c0:], c0, WIDTH, STEP)
            inv_v[c0 : c0 + WIDTH] = done
            if c0 + WIDTH < 128:
                inv_v[c0 + WIDTH :] = rest
        elif kind == "W":
            inv_v[...] = lower(inv_v[...])
            factor_ref[...] = fac_v[...]
            w_v[...] = fold3(
                lax.dot_general(split3(inv_v[...]), q_v[...], nt, preferred_element_type=F32)
            )
        elif kind == "S":
            csl = pl.ds(n * BLOCK, BLOCK)
            s_ref[:, csl] = jnp.dot(
                inv_v[...], t_sum[:, csl], precision=lax.Precision.HIGHEST,
                preferred_element_type=F32,
            )
            part = lax.dot_general(
                s_ref[:, csl], w_v[:, csl], nt, precision=lax.Precision.HIGHEST,
                preferred_element_type=F32,
            )
            g2[core] = part if n == 0 else g2[core] + part
        else:
            advance(n, "ABCD".index(kind))

    g2_copy = pltpu.make_async_remote_copy(
        src_ref=g2.at[core], dst_ref=g2.at[core], send_sem=hs_sem.at[1], recv_sem=hr_sem.at[1],
        device_id=sibling, device_id_type=MESH,
    )
    g2_copy.start()
    for i in range(n_chunk):
        p_copy(i).wait_send()
    for b in range(n_block):
        for stage in range(4):
            for offset in offsets(stage):
                send(b, stage, offset).wait_send()
    for stage in range(3):
        for offset in range(1, 4):
            gram_send(stage, offset).wait_send()
    gram_half().wait_send()
    g2_copy.wait()
    gram_ref[...] = g2[0] + g2[1]


def eliminate(rest, factor, c0, width, step):
    size = rest.shape[1]
    done = []
    for start in range(c0, c0 + width, step):
        n = rest.shape[0]
        lane = lax.broadcasted_iota(jnp.int32, (n, size), 1)
        row = lax.broadcasted_iota(jnp.int32, (n, size), 0)
        cols = [jnp.broadcast_to(rest[:, start + k : start + k + 1], (n, size)) for k in range(step)]
        eye = jnp.where(lane == row + start, 1.0, 0.0).astype(F32)
        rest = jnp.where((lane >= start) & (lane < start + step), eye, rest)
        scale = jnp.zeros((step, size), F32)
        part = jnp.zeros((n, size), F32)
        for k in range(step):
            pivot = cols[k][k : k + 1]
            root = lax.rsqrt(pivot)
            scale = jnp.where(row[:step] == k, root, scale)
            if factor is not None:
                part = jnp.where((lane == start + k) & (row >= k), cols[k] * root, part)
            mult = jnp.where(row > k, cols[k] * (1.0 / pivot), 0.0)
            for later in range(k + 1, step):
                cols[later] = cols[later] - mult * cols[later][k : k + 1]
            rest = rest - mult * rest[k : k + 1]
        if factor is not None:
            ahead = factor.shape[0] - n
            factor = factor + part if not ahead else jnp.concatenate(
                [factor[:ahead], factor[ahead:] + part], 0
            )
        done.append(rest[:step] * scale)
        rest = rest[step:]
    return jnp.concatenate(done, 0), rest, factor


def terms3(x):
    high = x.astype(BF16)
    rest = x - high.astype(F32)
    mid = rest.astype(BF16)
    return high, mid, (rest - mid.astype(F32)).astype(BF16)


def split3(x):
    return jnp.concatenate(terms3(x), 0)


def fold3(x):
    n = x.shape[0] // 3
    return x[0:n] + (x[n : 2 * n] + x[2 * n :])


def inverse_by_blocks(rest, step):
    size = rest.shape[0]
    lane = lax.broadcasted_iota(jnp.int32, (size, size), 1)
    row = lax.broadcasted_iota(jnp.int32, (step, size), 0)
    done = []
    for start in range(0, size, step):
        n = size - start
        block = (lane >= start) & (lane < start + step)

        def column(k, rows):
            return jnp.broadcast_to(rows[:, start + k : start + k + 1], rows.shape)

        cols = [column(k, rest[:step]) for k in range(step)]
        eye = jnp.where(lane[:step] == row + start, 1.0, 0.0).astype(F32)
        down = jnp.where(block[:step], eye, rest[:step])
        full = down
        pivots = []
        for k in range(step):
            pivots.append(cols[k][k : k + 1])
            mult = cols[k] * (1.0 / pivots[k])
            below = jnp.where(row > k, mult, 0.0)
            others = jnp.where(row != k, mult, 0.0)
            for later in range(k + 1, step):
                cols[later] = cols[later] - others * cols[later][k : k + 1]
            line = down[k : k + 1]
            down = down - below * line
            full = full - others * line
        pivots = jnp.concatenate(pivots, 0)
        done.append(down * lax.rsqrt(pivots))
        if n > step:
            full = full * (1.0 / pivots)
            terms = [column(k, rest[step:]) * full[k : k + 1] for k in range(step)]
            while len(terms) > 1:
                terms = [terms[i] + terms[i + 1] for i in range(0, len(terms), 2)]
            rest = jnp.where(block[: n - step], 0.0, rest[step:]) - terms[0]
    return lower(jnp.concatenate(done, 0))


def lower(x):
    lane = lax.broadcasted_iota(jnp.int32, x.shape, 1)
    row = lax.broadcasted_iota(jnp.int32, x.shape, 0)
    return jnp.where(lane <= row, x, 0.0)


def final_kernel(row_factor, s_ref, gram_ref, factor_ref, out_ref, scaled_ref, right_v):
    scaled_ref[...] = factor_ref[...] * row_factor
    high, mid, low = terms3(s_ref[...])
    for place, term in enumerate((high, mid, high, mid, low, high)):
        right_v[128 * place : 128 * (place + 1)] = term
    gram = gram_ref[...]
    inverse = inverse_by_blocks(0.5 * (gram + gram.T), 2 * STEP) * row_factor
    high, mid, low = terms3(inverse)
    left = jnp.concatenate([high, high, mid, mid, high, low], 1)
    out_ref[...] = jnp.dot(left, right_v[...], preferred_element_type=F32).T


def on_device(embeddings, start_basis):
    rows, cols = embeddings.shape
    k = start_basis.shape[1]
    n_block = cols // BLOCK
    n_chunk = rows // CHUNK
    row_factor = (rows * lax.axis_size("dp")) ** (-0.5)
    vmem = pl.BlockSpec(memory_space=pltpu.VMEM)
    anywhere = pl.BlockSpec(memory_space=pltpu.HBM)
    dma = pltpu.SemaphoreType.DMA
    whitened, gram, factor = pl.pallas_call(
        reduce_kernel,
        out_shape=[
            jax.ShapeDtypeStruct((k, cols), F32),
            jax.ShapeDtypeStruct((k, k), F32),
            jax.ShapeDtypeStruct((k, k), F32),
        ],
        in_specs=[anywhere, anywhere],
        out_specs=[vmem, vmem, vmem],
        scratch_shapes=[
            pltpu.VMEM((rows, cols), BF16),
            pltpu.VMEM((cols, k), BF16),
            pltpu.VMEM((rows, k), F32),
            pltpu.VMEM((rows, k), F32),
            pltpu.VMEM((2 * k, rows), BF16),
            pltpu.VMEM((k, cols), F32),
            pltpu.VMEM((k, cols), F32),
            pltpu.VMEM((n_block, 3, 32, BLOCK), F32),
            pltpu.VMEM((n_block, 15, 8, 128), F32),
            pltpu.VMEM((n_block, 32, BLOCK), F32),
            pltpu.VMEM((3, 4, k // 2, k), F32),
            pltpu.VMEM((3, k // 2, k), F32),
            pltpu.VMEM((2, k // 2, k), F32),
            pltpu.VMEM((k, k), F32),
            pltpu.VMEM((k, k), F32),
            pltpu.VMEM((k, cols), F32),
            pltpu.VMEM((2, k, k), F32),
            dma((n_chunk,)), dma, dma((n_chunk,)), dma((n_chunk,)),
            dma((n_block, 36)), dma((n_block, 36)),
            dma((3, 3)), dma((3, 3)), dma((2,)), dma((2,)),
        ],
        compiler_params=pltpu.CompilerParams(
            collective_id=0, has_side_effects=True, vmem_limit_bytes=52 * 2**20
        ),
        name="image_and_sum",
    )(embeddings, pltpu.with_memory_space_constraint(start_basis, pltpu.HBM))
    return tuple(
        pl.pallas_call(
            functools.partial(final_kernel, row_factor),
            out_shape=[
                jax.ShapeDtypeStruct((cols, k), F32),
                jax.ShapeDtypeStruct((k, k), F32),
            ],
            in_specs=[vmem, vmem, vmem],
            out_specs=[vmem, vmem],
            scratch_shapes=[pltpu.VMEM((6 * k, cols), BF16)],
            compiler_params=pltpu.CompilerParams(vmem_limit_bytes=32 * 2**20),
            name="final",
        )(whitened, gram, factor)
    )


def solution(mesh):
    placed = (P("dp", "col"), P("col", None))
    return jax.shard_map(
        on_device, mesh=mesh, in_specs=placed, out_specs=(P("col", None), P()), check_vma=False
    )
```
